128 devices in a mesh: pair: 8 (over y, x_hi), mat: 16 (over x_lo, z, core).
Axes of the slice: x: 4 (x_hi: 2, x_lo: 2; x = x_hi * 2 + x_lo), y: 4, z: 4, core: 2. Of those that a mesh axis runs over, the one named last changes fastest.
Arguments:
- operators: bfloat16 [32, 2048, 2048], P('pair', 'mat'), may hold values from -6 to 6
- left_rot: bfloat16 [2048, 2048], P('mat'), may hold values from -0.125 to 0.125
- right_rot: bfloat16 [2048, 2048], P('mat'), may hold values from -0.125 to 0.125
- integrals: float32 [1024, 1024], replicated, may hold values from -1.0606601 to 1.0606601
- pair_index: int32 [32], replicated, may hold values from 0 to 1023
- target_index: int32 [32], replicated, may hold values from 0 to 1023
Outputs:
- complement: bfloat16 [32, 2048, 2048], P('pair', None, 'mat')
The draws below stay inside these ranges and needn't reach their ends.
All inputs are finite; a program needn't handle non-finite values.
Results may differ from the reference program's by a relative error of at most 0.0063.
Values may be sent and summed in bfloat16 or wider, within the bound.
No kernel may reach another device: no remote copies, remote signals or barrier semaphores. Data moves between devices by JAX's collectives and lax.ppermute only.
A program may use at most 192 MiB of HBM per device.

```python
import jax
import jax.numpy as jnp
from jax import lax

M = 2048
NPQ = 1024
NSEL = 32
NTGT = 32


def set_ends(values, key, least, high):
    shape = values.shape
    spot = [jax.random.randint(jax.random.fold_in(key, axis), (), 0, shape[axis]) for axis in range(len(shape))]
    values = values.at[tuple(spot)].set(least)
    longest = shape.index(max(shape))
    spot[longest] = (spot[longest] + 1) % shape[longest]
    return values.at[tuple(spot)].set(high)


def shard_levels(stream_key, dims, shards, least, high):
    gain = 1.0
    for position, shards_of in shards:
        heights = jax.random.uniform(jax.random.fold_in(jax.random.fold_in(stream_key, 6), position), (shards_of,), jnp.float32, least / len(shards), high / len(shards))
        gain = gain * jnp.repeat(jnp.exp(heights), dims[position] // shards_of).reshape((-1,) + (1,) * (len(dims) - 1 - position))
    return gain


def centred(rng, shape, width, limit, pieces=(), held_as=jnp.bfloat16):
    result = width * jax.random.normal(rng, shape, jnp.float32)
    if pieces:
        result = result * shard_levels(rng, shape, pieces, -0.22, 0.18)
    return jnp.clip(result, -limit, limit).astype(held_as)


def setup_inputs(seed: int = 0) -> dict:
    keys = jax.random.split(jax.random.key(seed), 7)
    operators = centred(keys[0], (NSEL, M, M), 1.0, 6.0, ((0, 8), (1, 16)))
    left_rot = centred(keys[1], (M, M), M ** -0.5, 0.125, ((0, 16),))
    right_rot = centred(keys[2], (M, M), M ** -0.5, 0.125, ((0, 16),))
    integrals = centred(keys[3], (NPQ, NPQ), (NSEL ** -0.5), 1.0606601, (), jnp.float32)
    pair_index = set_ends(jax.random.randint(keys[4], (NSEL,), 0, NPQ), jax.random.fold_in(keys[4], 1), 0, NPQ - 1).astype(jnp.int32)
    target_index = set_ends(jax.random.randint(keys[5], (NTGT,), 0, NPQ), jax.random.fold_in(keys[5], 1), 0, NPQ - 1).astype(jnp.int32)
    return dict(operators=operators, left_rot=left_rot, right_rot=right_rot, integrals=integrals, pair_index=pair_index, target_index=target_index)


def rotate_one(single, left_rot, right_rot):
    half_rot = jnp.dot(single, right_rot, preferred_element_type=jnp.float32).astype(jnp.bfloat16)
    return jnp.dot(left_rot.T, half_rot, preferred_element_type=jnp.float32).astype(jnp.bfloat16)


def reference(operators, left_rot, right_rot, integrals, pair_index, target_index):
    rotated = lax.map(lambda single: rotate_one(single, left_rot, right_rot), operators)
    coupling = integrals[target_index.astype(jnp.int32)][:, pair_index.astype(jnp.int32)].astype(jnp.bfloat16)
    weights = coupling.astype(jnp.float32)

    def assemble(row_weights):
        return jnp.einsum("k,kmn->mn", row_weights, rotated.astype(jnp.float32)).astype(jnp.bfloat16)

    return lax.map(assemble, weights)
```

```python
import jax
import jax.numpy as jnp
from jax import lax
from jax.sharding import Mesh, PartitionSpec as P

AXES = ("y", "xh", "xl", "z", "core")
PAIR = ("y", "xh")
MAT = ("xl", "z", "core")


def selector(indices, count):
    return (indices[:, None] == jnp.arange(count, dtype=jnp.int32)[None, :]).astype(jnp.float32)


def shards(operators, left_rot, right_rot, integrals, pair_index, target_index):
    right = lax.all_gather(right_rot, MAT, axis=0, tiled=True)
    left = lax.all_gather(left_rot, MAT, axis=0, tiled=True)
    pieces = operators.reshape(4, 8, 16, 2048).transpose(1, 0, 2, 3)
    pieces = lax.all_to_all(pieces, PAIR, 0, 0, tiled=True).reshape(512, 2048)
    npairs = integrals.shape[0]
    rowsel = jnp.dot(selector(target_index, npairs), integrals, precision=lax.Precision.HIGHEST)
    coupling = jnp.dot(
        rowsel, selector(pair_index, npairs).T, precision=lax.Precision.HIGHEST
    ).astype(jnp.bfloat16)
    spread = (coupling[:, None, :, None] * jnp.eye(16, dtype=jnp.bfloat16)[None, :, None, :]).reshape(512, 512)
    mixed = jnp.dot(spread, pieces, preferred_element_type=jnp.float32).astype(jnp.bfloat16)
    half = jnp.dot(mixed, right, preferred_element_type=jnp.float32).astype(jnp.bfloat16)
    blocks = half.reshape(8, 64, 16, 128).transpose(0, 2, 1, 3).reshape(128, 64, 128)
    columns = lax.all_to_all(blocks, AXES, 0, 0, tiled=True)
    columns = columns.reshape(8, 16, 4, 16, 128).transpose(2, 1, 0, 3, 4).reshape(4, 2048, 128)
    out = jnp.einsum("rm,trc->tmc", left, columns, preferred_element_type=jnp.float32)
    return out.astype(jnp.bfloat16)


def solution(mesh):
    fine = Mesh(mesh.devices.reshape(4, 2, 2, 4, 2), AXES)
    in_specs = (P(PAIR, MAT, None), P(MAT, None), P(MAT, None), P(), P(), P())
    out_specs = P(PAIR, None, MAT)
    return jax.shard_map(shards, mesh=fine, in_specs=in_specs, out_specs=out_specs, check_vma=False)
```

```python
import jax
import jax.numpy as jnp
from jax import lax
from jax.experimental import pallas as pl
from jax.experimental.pallas import tpu as pltpu
from jax.sharding import Mesh, PartitionSpec as P

AXES = ("y", "xh", "xl", "z", "core")
PAIR = ("y", "xh")
MAT = ("xl", "z", "core")
BF = jnp.bfloat16
F32 = jnp.float32
HALF, FINAL = 56, 56


def place(x, y, z, core):
    x, y, z = x % 4, y % 4, z % 4
    return (y * 2 + x // 2) * 16 + ((x % 2) * 4 + z) * 2 + core


def send(value, move):
    moves = [
        (place(x, y, z, core), place(*move(x, y, z, core)))
        for x in range(4)
        for y in range(4)
        for z in range(4)
        for core in range(2)
    ]
    return lax.ppermute(value, AXES, moves)


def swap_core(value):
    return send(value, lambda x, y, z, core: (x, y, z, 1 - core))


def shift(value, dx=0, dy=0, dz=0):
    def move(x, y, z, core):
        way = 1 - 2 * core
        return x + way * dx, y + way * dy, z + way * dz, core

    return send(value, move)


def selector(indices, count):
    return (indices[:, None] == jnp.arange(count, dtype=jnp.int32)[None, :]).astype(F32)


def spread_coupling(integrals, pair_index, target_index):
    npairs = integrals.shape[0]
    rowsel = jnp.dot(selector(target_index, npairs), integrals, precision=lax.Precision.HIGHEST)
    coupling = jnp.dot(rowsel, selector(pair_index, npairs).T, precision=lax.Precision.HIGHEST).astype(BF)
    wide = selector(jnp.arange(512, dtype=jnp.int32) // 16, 32).astype(BF)
    rows = jnp.dot(wide, coupling, preferred_element_type=F32).astype(BF)
    full = jnp.dot(rows, wide.T, preferred_element_type=F32).astype(BF)
    i = lax.broadcasted_iota(jnp.int32, (512, 512), 0) % 16
    j = lax.broadcasted_iota(jnp.int32, (512, 512), 1) % 16
    return jnp.where(i == j, full, jnp.zeros_like(full))


def mix_kernel(spread, *refs):
    *parts, out = refs
    width = out.shape[1] // len(parts)
    for n, part in enumerate(parts):
        out[:, n * width : (n + 1) * width] = jnp.dot(spread[...], part[...], preferred_element_type=F32).astype(BF)


def mix(spread, parts):
    return pl.pallas_call(
        mix_kernel,
        out_shape=jax.ShapeDtypeStruct((512, 2048), BF),
        compiler_params=pltpu.CompilerParams(vmem_limit_bytes=16 << 20),
        name="mix",
    )(spread, *parts)


def half_kernel(order, rows, *refs):
    *rights, out, natural = refs
    for n, right in enumerate(rights):
        natural[pl.ds(pl.multiple_of(order[n] * 128, 128), 128), :] = right[...]
    total = jnp.dot(rows[...], natural[...], preferred_element_type=F32).astype(BF)
    for p in range(8):
        for m in range(out.shape[1]):
            for t in range(4):
                top = (p * 4 + t) * 16
                out[p, m, :, t * 128 : t * 128 + 128] = total[top : top + 16, m * 128 : m * 128 + 128]


def half_rotate(order, rows, rights):
    width = 512
    return pl.pallas_call(
        half_kernel,
        grid_spec=pltpu.PrefetchScalarGridSpec(
            num_scalar_prefetch=1,
            grid=(2048 // width,),
            in_specs=[pl.BlockSpec((512, 2048), lambda i, o: (0, 0))]
            + [pl.BlockSpec((128, width), lambda i, o: (0, i)) for _ in rights],
            out_specs=pl.BlockSpec((8, width // 128, 16, 512), lambda i, o: (0, i, 0, 0)),
            scratch_shapes=[pltpu.VMEM((2048, width), BF)],
        ),
        out_shape=jax.ShapeDtypeStruct((8, 16, 16, 512), BF),
        compiler_params=pltpu.CompilerParams(vmem_limit_bytes=HALF << 20),
        name="half",
    )(order, rows, *rights)


def final_kernel(order, *refs):
    *lefts, columns, out, rows = refs

    @pl.when(pl.program_id(0) == 0)
    def _():
        for n in range(len(lefts)):
            for chip in range(4):
                for p in range(2):
                    top = n * 128 + chip * 32 + p * 16
                    pair, place = order[2 * n] * 2 + p, order[2 * len(lefts) + (n // 4) * 4 + chip]
                    rows[top : top + 16, :] = columns[pair, place]

    left = jnp.concatenate([piece[...] for piece in lefts], axis=0)
    total = lax.dot_general(left, rows[...], (((0,), (0,)), ((), ())), preferred_element_type=F32).astype(BF)
    for t in range(4):
        out[t] = total[:, t * 128 : t * 128 + 128]


def final_rotate(order, lefts, columns):
    height = 512
    return pl.pallas_call(
        final_kernel,
        grid_spec=pltpu.PrefetchScalarGridSpec(
            num_scalar_prefetch=1,
            grid=(2048 // height,),
            in_specs=[pl.BlockSpec((128, height), lambda i, o: (0, i)) for _ in lefts]
            + [pl.BlockSpec((8, 16, 16, 512), lambda i, o: (0, 0, 0, 0))],
            out_specs=pl.BlockSpec((4, height, 128), lambda i, o: (0, i, 0)),
            scratch_shapes=[pltpu.VMEM((2048, 512), BF)],
        ),
        out_shape=jax.ShapeDtypeStruct((4, 2048, 128), BF),
        compiler_params=pltpu.CompilerParams(vmem_limit_bytes=FINAL << 20),
        name="final",
    )(order, *lefts, columns)


def after(*values):
    return lax.optimization_barrier(values)


def shards(operators, left_rot, right_rot, integrals, pair_index, target_index):
    core = lax.axis_index("core")
    y, xl, z = lax.axis_index("y"), lax.axis_index("xl"), lax.axis_index("z")

    near = [right_rot] + [shift(right_rot, dz=dz) for dz in (1, -1, 2)]
    there = shift(right_rot, dx=1)
    rights = near + [there, shift(there, dz=1), shift(there, dz=-1), shift(near[3], dx=1)]
    left_rot, there = after(left_rot, there)
    quarter = lax.dynamic_slice_in_dim(left_rot, y * 32, 32, 0)
    strip = jnp.concatenate([quarter, shift(quarter, dz=1), shift(quarter, dz=-1), shift(quarter, dz=2)])
    pieces = operators.reshape(4, 8, 16, 2048).transpose(1, 0, 2, 3)
    pieces = lax.all_to_all(pieces, PAIR, 0, 0, tiled=True).reshape(512, 2048)
    spread = spread_coupling(integrals, pair_index, target_index)
    lefts = [strip, shift(strip, dy=1), shift(strip, dy=-1), shift(strip, dy=2)]
    rights += [swap_core(right) for right in rights]

    rows = mix(spread, [pieces])

    def along_z(xl, core):
        way = 1 - 2 * core
        return [(xl * 4 + chip % 4) * 2 + core for chip in (z, z + 4 - way, z + 4 + way, z + 2)]

    places = along_z(xl, core) + along_z(1 - xl, core) + along_z(xl, 1 - core) + along_z(1 - xl, 1 - core)
    half = half_rotate(jnp.stack(places), rows, rights)
    across = shift(strip, dx=1)
    *lefts, across, half = after(*lefts, across, half)
    columns = lax.all_to_all(half.reshape(128, 16, 512), AXES, 0, 0, tiled=True)
    lefts += [across, shift(lefts[1], dx=1), shift(across, dy=-1), shift(lefts[3], dx=1)]
    lefts += [swap_core(left) for left in lefts]
    return final_rotate(jnp.stack(left_order(y, core) + places), lefts, columns.reshape(8, 16, 16, 512))


def left_order(y, core):
    order = []
    for side in (core, 1 - core):
        way = 1 - 2 * side
        for _ in range(2):
            for row in (y, (y + 4 - way) % 4, (y + 4 + way) % 4, (y + 2) % 4):
                order += [row, row]
    return order


def solution(mesh):
    fine = Mesh(mesh.devices.reshape(4, 2, 2, 4, 2), AXES)
    in_specs = (P(PAIR, MAT, None), P(MAT, None), P(MAT, None), P(), P(), P())
    out_specs = P(PAIR, None, MAT)
    return jax.shard_map(shards, mesh=fine, in_specs=in_specs, out_specs=out_specs, check_vma=False)
```

```python
import jax
import jax.numpy as jnp
from jax import lax
from jax.experimental import pallas as pl
from jax.experimental.pallas import tpu as pltpu
from jax.sharding import Mesh, PartitionSpec as P

AXES = ("y", "xh", "xl", "z", "core")
PAIR = ("y", "xh")
MAT = ("xl", "z", "core")
BF = jnp.bfloat16
F32 = jnp.float32
HALF, FINAL = 56, 56


def place(x, y, z, core):
    x, y, z = x % 4, y % 4, z % 4
    return (y * 2 + x // 2) * 16 + ((x % 2) * 4 + z) * 2 + core


def send(value, move):
    moves = [
        (place(x, y, z, core), place(*move(x, y, z, core)))
        for x in range(4)
        for y in range(4)
        for z in range(4)
        for core in range(2)
    ]
    return lax.ppermute(value, AXES, moves)


def swap_core(value):
    return send(value, lambda x, y, z, core: (x, y, z, 1 - core))


def shift(value, dx=0, dy=0, dz=0):
    def move(x, y, z, core):
        way = 1 - 2 * core
        return x + way * dx, y + way * dy, z + way * dz, core

    return send(value, move)


def selector(indices, count):
    return (indices[:, None] == jnp.arange(count, dtype=jnp.int32)[None, :]).astype(F32)


def spread_coupling(integrals, pair_index, target_index):
    npairs = integrals.shape[0]
    rowsel = jnp.dot(selector(target_index, npairs), integrals, precision=lax.Precision.HIGHEST)
    coupling = jnp.dot(rowsel, selector(pair_index, npairs).T, precision=lax.Precision.HIGHEST).astype(BF)
    wide = selector(jnp.arange(512, dtype=jnp.int32) // 16, 32).astype(BF)
    rows = jnp.dot(wide, coupling, preferred_element_type=F32).astype(BF)
    full = jnp.dot(rows, wide.T, preferred_element_type=F32).astype(BF)
    i = lax.broadcasted_iota(jnp.int32, (512, 512), 0) % 16
    j = lax.broadcasted_iota(jnp.int32, (512, 512), 1) % 16
    return jnp.where(i == j, full, jnp.zeros_like(full))


def mix_kernel(spread, *refs):
    *parts, out = refs
    width = out.shape[1] // len(parts)
    for n, part in enumerate(parts):
        out[:, n * width : (n + 1) * width] = jnp.dot(spread[...], part[...], preferred_element_type=F32).astype(BF)


def mix(spread, parts):
    return pl.pallas_call(
        mix_kernel,
        out_shape=jax.ShapeDtypeStruct((512, 2048), BF),
        compiler_params=pltpu.CompilerParams(vmem_limit_bytes=16 << 20),
        name="mix",
    )(spread, *parts)


def half_kernel(order, rows, *refs):
    *rights, out, natural = refs
    for n, right in enumerate(rights):
        natural[pl.ds(pl.multiple_of(order[n] * 128, 128), 128), :] = right[...]
    total = jnp.dot(rows[...], natural[...], preferred_element_type=F32).astype(BF)
    for p in range(8):
        for m in range(out.shape[1]):
            for t in range(4):
                top = (p * 4 + t) * 16
                out[p, m, :, t * 128 : t * 128 + 128] = total[top : top + 16, m * 128 : m * 128 + 128]


def half_rotate(order, rows, rights):
    width = 512
    return pl.pallas_call(
        half_kernel,
        grid_spec=pltpu.PrefetchScalarGridSpec(
            num_scalar_prefetch=1,
            grid=(2048 // width,),
            in_specs=[pl.BlockSpec((512, 2048), lambda i, o: (0, 0))]
            + [pl.BlockSpec((128, width), lambda i, o: (0, i)) for _ in rights],
            out_specs=pl.BlockSpec((8, width // 128, 16, 512), lambda i, o: (0, i, 0, 0)),
            scratch_shapes=[pltpu.VMEM((2048, width), BF)],
        ),
        out_shape=jax.ShapeDtypeStruct((8, 16, 16, 512), BF),
        compiler_params=pltpu.CompilerParams(vmem_limit_bytes=HALF << 20),
        name="half",
    )(order, rows, *rights)


def final_kernel(order, *refs):
    *lefts, columns, out, rows = refs

    @pl.when(pl.program_id(0) == 0)
    def _():
        for n in range(len(lefts)):
            for chip in range(4):
                for p in range(2):
                    top = n * 128 + chip * 32 + p * 16
                    pair, place = order[2 * n] * 2 + p, order[2 * len(lefts) + (n // 4) * 4 + chip]
                    rows[top : top + 16, :] = columns[pair, place]

    left = jnp.concatenate([piece[...] for piece in lefts], axis=0)
    total = lax.dot_general(left, rows[...], (((0,), (0,)), ((), ())), preferred_element_type=F32).astype(BF)
    for t in range(4):
        out[t] = total[:, t * 128 : t * 128 + 128]


def final_rotate(order, lefts, columns):
    height = 512
    return pl.pallas_call(
        final_kernel,
        grid_spec=pltpu.PrefetchScalarGridSpec(
            num_scalar_prefetch=1,
            grid=(2048 // height,),
            in_specs=[pl.BlockSpec((128, height), lambda i, o: (0, i)) for _ in lefts]
            + [pl.BlockSpec((8, 16, 16, 512), lambda i, o: (0, 0, 0, 0))],
            out_specs=pl.BlockSpec((4, height, 128), lambda i, o: (0, i, 0)),
            scratch_shapes=[pltpu.VMEM((2048, 512), BF)],
        ),
        out_shape=jax.ShapeDtypeStruct((4, 2048, 128), BF),
        compiler_params=pltpu.CompilerParams(vmem_limit_bytes=FINAL << 20),
        name="final",
    )(order, *lefts, columns)


def after(*values):
    return lax.optimization_barrier(values)


def shards(operators, left_rot, right_rot, integrals, pair_index, target_index):
    core = lax.axis_index("core")
    y, xl, z = lax.axis_index("y"), lax.axis_index("xl"), lax.axis_index("z")

    near = [right_rot] + [shift(right_rot, dz=dz) for dz in (1, -1, 2)]
    there = shift(right_rot, dx=1)
    pieces = operators.reshape(4, 8, 16, 2048).transpose(1, 0, 2, 3)
    pieces = lax.all_to_all(pieces, PAIR, 0, 0, tiled=True).reshape(512, 2048)
    spread = spread_coupling(integrals, pair_index, target_index)
    left_rot, there, spread = after(left_rot, there, spread)
    quarter = lax.dynamic_slice_in_dim(left_rot, y * 32, 32, 0)
    strip = jnp.concatenate([quarter, shift(quarter, dz=1), shift(quarter, dz=-1), shift(quarter, dz=2)])
    rights = near + [there, shift(there, dz=1), shift(there, dz=-1), shift(near[3], dx=1)]
    rights += [swap_core(right) for right in rights]
    rows = mix(spread, [pieces])
    rows, strip, *rights = after(rows, strip, *rights)
    lefts = [strip, shift(strip, dy=1), shift(strip, dy=-1)]

    def along_z(xl, core):
        way = 1 - 2 * core
        return [(xl * 4 + chip % 4) * 2 + core for chip in (z, z + 4 - way, z + 4 + way, z + 2)]

    places = along_z(xl, core) + along_z(1 - xl, core) + along_z(xl, 1 - core) + along_z(1 - xl, 1 - core)
    half = half_rotate(jnp.stack(places), rows, rights)
    lefts.append(shift(lefts[1], dy=1))
    lefts += [shift(left, dx=1) for left in lefts[:3]]
    columns = lax.all_to_all(half.reshape(128, 16, 512), AXES, 0, 0, tiled=True)
    lefts.append(shift(lefts[3], dx=1))
    lefts += [swap_core(left) for left in lefts]
    return final_rotate(jnp.stack(left_order(y, core) + places), lefts, columns.reshape(8, 16, 16, 512))


def left_order(y, core):
    order = []
    for side in (core, 1 - core):
        way = 1 - 2 * side
        for _ in range(2):
            for row in (y, (y + 4 - way) % 4, (y + 4 + way) % 4, (y + 2) % 4):
                order += [row, row]
    return order


def solution(mesh):
    fine = Mesh(mesh.devices.reshape(4, 2, 2, 4, 2), AXES)
    in_specs = (P(PAIR, MAT, None), P(MAT, None), P(MAT, None), P(), P(), P())
    out_specs = P(PAIR, None, MAT)
    return jax.shard_map(shards, mesh=fine, in_specs=in_specs, out_specs=out_specs, check_vma=False)
```

```python
import jax
import jax.numpy as jnp
from jax import lax
from jax.experimental import pallas as pl
from jax.experimental.pallas import tpu as pltpu
from jax.sharding import Mesh, PartitionSpec as P

AXES = ("y", "xh", "xl", "z", "core")
PAIR = ("y", "xh")
MAT = ("xl", "z", "core")
BF = jnp.bfloat16
F32 = jnp.float32
HALF, FINAL = 56, 56


def place(x, y, z, core):
    x, y, z = x % 4, y % 4, z % 4
    return (y * 2 + x // 2) * 16 + ((x % 2) * 4 + z) * 2 + core


def send(value, move):
    moves = [
        (place(x, y, z, core), place(*move(x, y, z, core)))
        for x in range(4)
        for y in range(4)
        for z in range(4)
        for core in range(2)
    ]
    return lax.ppermute(value, AXES, moves)


def swap_core(value):
    return send(value, lambda x, y, z, core: (x, y, z, 1 - core))


def shift(value, dx=0, dy=0, dz=0):
    def move(x, y, z, core):
        way = 1 - 2 * core
        return x + way * dx, y + way * dy, z + way * dz, core

    return send(value, move)


def selector(indices, count):
    return (indices[:, None] == jnp.arange(count, dtype=jnp.int32)[None, :]).astype(F32)


def spread_coupling(integrals, pair_index, target_index):
    npairs = integrals.shape[0]
    rowsel = jnp.dot(selector(target_index, npairs), integrals, precision=lax.Precision.HIGHEST)
    coupling = jnp.dot(rowsel, selector(pair_index, npairs).T, precision=lax.Precision.HIGHEST).astype(BF)
    wide = selector(jnp.arange(512, dtype=jnp.int32) // 16, 32).astype(BF)
    rows = jnp.dot(wide, coupling, preferred_element_type=F32).astype(BF)
    full = jnp.dot(rows, wide.T, preferred_element_type=F32).astype(BF)
    i = lax.broadcasted_iota(jnp.int32, (512, 512), 0) % 16
    j = lax.broadcasted_iota(jnp.int32, (512, 512), 1) % 16
    return jnp.where(i == j, full, jnp.zeros_like(full))


def mix_kernel(spread, *refs):
    *parts, out = refs
    width = out.shape[1] // len(parts)
    for n, part in enumerate(parts):
        out[:, n * width : (n + 1) * width] = jnp.dot(spread[...], part[...], preferred_element_type=F32).astype(BF)


def mix(spread, parts):
    return pl.pallas_call(
        mix_kernel,
        out_shape=jax.ShapeDtypeStruct((512, 2048), BF),
        compiler_params=pltpu.CompilerParams(vmem_limit_bytes=16 << 20),
        name="mix",
    )(spread, *parts)


def half_kernel(order, rows, *refs):
    *rights, out, natural = refs
    for n, right in enumerate(rights):
        natural[pl.ds(pl.multiple_of(order[n] * 128, 128), 128), :] = right[...]
    total = jnp.dot(rows[...].reshape(256, 2048), natural[...], preferred_element_type=F32).astype(BF)
    for p in range(8):
        for m in range(out.shape[1]):
            for t in range(2):
                top = (p * 2 + t) * 16
                out[p, m, :, t * 128 : t * 128 + 128] = total[top : top + 16, m * 128 : m * 128 + 128]


def half_rotate(order, rows, rights, part):
    width = 512
    return pl.pallas_call(
        half_kernel,
        grid_spec=pltpu.PrefetchScalarGridSpec(
            num_scalar_prefetch=1,
            grid=(2048 // width,),
            in_specs=[pl.BlockSpec((8, 2, 16, 2048), lambda i, o: (0, part, 0, 0))]
            + [pl.BlockSpec((128, width), lambda i, o: (0, i)) for _ in rights],
            out_specs=pl.BlockSpec((8, width // 128, 16, 256), lambda i, o: (0, i, 0, 0)),
            scratch_shapes=[pltpu.VMEM((2048, width), BF)],
        ),
        out_shape=jax.ShapeDtypeStruct((8, 16, 16, 256), BF),
        compiler_params=pltpu.CompilerParams(vmem_limit_bytes=HALF << 20),
        name="half",
    )(order, rows, *rights)


def final_kernel(order, *refs):
    lefts, (columns, *_, out, rows) = refs[:16], refs[16:]

    @pl.when(pl.program_id(0) == 0)
    def _():
        for n in range(len(lefts)):
            for chip in range(4):
                for p in range(2):
                    top = n * 128 + chip * 32 + p * 16
                    pair, place = order[2 * n] * 2 + p, order[2 * len(lefts) + (n // 4) * 4 + chip]
                    rows[top : top + 16, :] = columns[pair, place]

    left = jnp.concatenate([piece[...] for piece in lefts], axis=0)
    total = lax.dot_general(left, rows[...], (((0,), (0,)), ((), ())), preferred_element_type=F32).astype(BF)
    for t in range(2):
        out[t] = total[:, t * 128 : t * 128 + 128]


def final_rotate(order, lefts, columns, part, begun=()):
    height = 512
    return pl.pallas_call(
        final_kernel,
        grid_spec=pltpu.PrefetchScalarGridSpec(
            num_scalar_prefetch=1,
            grid=(2048 // height,),
            in_specs=[pl.BlockSpec((128, height), lambda i, o: (0, i)) for _ in lefts]
            + [pl.BlockSpec((8, 16, 16, 256), lambda i, o: (0, 0, 0, 0))]
            + [pl.BlockSpec(memory_space=pl.ANY) for _ in begun],
            out_specs=pl.BlockSpec((2, height, 128), lambda i, o: (part, i, 0)),
            scratch_shapes=[pltpu.VMEM((2048, 256), BF)],
        ),
        out_shape=jax.ShapeDtypeStruct((4, 2048, 128), BF),
        input_output_aliases={18: 0} if begun else {},
        compiler_params=pltpu.CompilerParams(vmem_limit_bytes=FINAL << 20),
        cost_estimate=pl.CostEstimate(flops=2 * 256 * 2048 * 2048, bytes_accessed=10 << 20, transcendentals=0),
        name="final",
    )(order, *lefts, columns, *begun)


def after(*values):
    return lax.optimization_barrier(values)


def shards(operators, left_rot, right_rot, integrals, pair_index, target_index):
    core = lax.axis_index("core")
    y, xl, z = lax.axis_index("y"), lax.axis_index("xl"), lax.axis_index("z")

    near = [right_rot] + [shift(right_rot, dz=dz) for dz in (1, -1, 2)]
    there = shift(right_rot, dx=1)
    pieces = operators.reshape(4, 8, 16, 2048).transpose(1, 0, 2, 3)
    pieces = lax.all_to_all(pieces, PAIR, 0, 0, tiled=True).reshape(512, 2048)
    spread = spread_coupling(integrals, pair_index, target_index)
    left_rot, there, spread = after(left_rot, there, spread)
    quarter = lax.dynamic_slice_in_dim(left_rot, y * 32, 32, 0)
    strip = jnp.concatenate([quarter, shift(quarter, dz=1), shift(quarter, dz=-1), shift(quarter, dz=2)])
    rights = near + [there, shift(there, dz=1), shift(there, dz=-1), shift(near[3], dx=1)]
    rights += [swap_core(right) for right in rights]
    rows = mix(spread, [pieces])
    rows, strip, *rights = after(rows.reshape(8, 4, 16, 2048), strip, *rights)
    lefts = [strip, shift(strip, dy=1), shift(strip, dy=-1)]
    across = [shift(strip, dx=1), shift(strip, dx=1, dy=1)]

    def along_z(xl, core):
        way = 1 - 2 * core
        return [(xl * 4 + chip % 4) * 2 + core for chip in (z, z + 4 - way, z + 4 + way, z + 2)]

    places = along_z(xl, core) + along_z(1 - xl, core) + along_z(xl, 1 - core) + along_z(1 - xl, 1 - core)
    def exchange(half):
        return lax.all_to_all(half.reshape(128, 16, 256), AXES, 0, 0, tiled=True).reshape(8, 16, 16, 256)

    places = jnp.stack(places)
    first = exchange(half_rotate(places, rows, rights, 0))
    rows, *lefts, across[0], across[1] = after(rows, *lefts, *across)
    half = half_rotate(places, rows, rights, 1)
    half, *lefts, across[0], across[1] = after(half, *lefts, *across)
    second = exchange(half)
    lefts.append(shift(lefts[1], dy=1))
    lefts += [across[0], across[1], shift(lefts[2], dx=1), shift(across[1], dy=1)]
    lefts += [swap_core(left) for left in lefts]
    order = jnp.concatenate([jnp.stack(left_order(y, core)), places])
    begun = final_rotate(order, lefts, first, 0)
    return final_rotate(order, lefts, second, 1, (begun,))


def left_order(y, core):
    order = []
    for side in (core, 1 - core):
        way = 1 - 2 * side
        for _ in range(2):
            for row in (y, (y + 4 - way) % 4, (y + 4 + way) % 4, (y + 2) % 4):
                order += [row, row]
    return order


def solution(mesh):
    fine = Mesh(mesh.devices.reshape(4, 2, 2, 4, 2), AXES)
    in_specs = (P(PAIR, MAT, None), P(MAT, None), P(MAT, None), P(), P(), P())
    out_specs = P(PAIR, None, MAT)
    return jax.shard_map(shards, mesh=fine, in_specs=in_specs, out_specs=out_specs, check_vma=False)
```

```python
import jax
import jax.numpy as jnp
from jax import lax
from jax.experimental import pallas as pl
from jax.experimental.pallas import tpu as pltpu
from jax.sharding import Mesh, PartitionSpec as P

AXES = ("y", "xh", "xl", "z", "core")
PAIR = ("y", "xh")
MAT = ("xl", "z", "core")
BF = jnp.bfloat16
F32 = jnp.float32
HALF, FINAL = 56, 16
SLICES = 2


def place(x, y, z, core):
    x, y, z = x % 4, y % 4, z % 4
    return (y * 2 + x // 2) * 16 + ((x % 2) * 4 + z) * 2 + core


def send(value, move):
    moves = [
        (place(x, y, z, core), place(*move(x, y, z, core)))
        for x in range(4)
        for y in range(4)
        for z in range(4)
        for core in range(2)
    ]
    return lax.ppermute(value, AXES, moves)


def swap_core(value):
    return send(value, lambda x, y, z, core: (x, y, z, 1 - core))


def shift(value, dx=0, dy=0, dz=0):
    def move(x, y, z, core):
        way = 1 - 2 * core
        return x + way * dx, y + way * dy, z + way * dz, core

    return send(value, move)


def selector(indices, count):
    return (indices[:, None] == jnp.arange(count, dtype=jnp.int32)[None, :]).astype(F32)


def spread_coupling(integrals, pair_index, target_index):
    npairs = integrals.shape[0]
    rowsel = jnp.dot(selector(target_index, npairs), integrals, precision=lax.Precision.HIGHEST)
    coupling = jnp.dot(rowsel, selector(pair_index, npairs).T, precision=lax.Precision.HIGHEST).astype(BF)
    wide = selector(jnp.arange(512, dtype=jnp.int32) // 16, 32).astype(BF)
    rows = jnp.dot(wide, coupling, preferred_element_type=F32).astype(BF)
    full = jnp.dot(rows, wide.T, preferred_element_type=F32).astype(BF)
    i = lax.broadcasted_iota(jnp.int32, (512, 512), 0) % 16
    j = lax.broadcasted_iota(jnp.int32, (512, 512), 1) % 16
    return jnp.where(i == j, full, jnp.zeros_like(full))


def mix_kernel(spread, *refs):
    *parts, out = refs
    width = out.shape[1] // len(parts)
    for n, part in enumerate(parts):
        out[:, n * width : (n + 1) * width] = jnp.dot(spread[...], part[...], preferred_element_type=F32).astype(BF)


def mix(spread, parts):
    return pl.pallas_call(
        mix_kernel,
        out_shape=jax.ShapeDtypeStruct((512, 2048), BF),
        compiler_params=pltpu.CompilerParams(vmem_limit_bytes=16 << 20),
        name="mix",
    )(spread, *parts)


def half_kernel(order, rows, *refs):
    rights, (out, natural, arrived) = refs[:16], refs[16:]
    width = 2048 // SLICES
    copies = [
        [
            pltpu.make_async_copy(
                right.at[:, part * width : (part + 1) * width],
                natural.at[pl.ds(pl.multiple_of(order[n] * 128, 128), 128), part * width : (part + 1) * width],
                arrived.at[part, n],
            )
            for n, right in enumerate(rights)
        ]
        for part in range(SLICES)
    ]
    for copy in sum(copies, []):
        copy.start()
    own = rows[...].reshape(256, 2048)
    for part in range(SLICES):
        for copy in copies[part]:
            copy.wait()
        for left in range(part * width, (part + 1) * width, 512):
            total = jnp.dot(own, natural[:, left : left + 512], preferred_element_type=F32).astype(BF)
            for p in range(8):
                for m in range(4):
                    for t in range(2):
                        top = (p * 2 + t) * 16
                        out[p, left // 128 + m, :, t * 128 : t * 128 + 128] = total[
                            top : top + 16, m * 128 : m * 128 + 128
                        ]


def half_rotate(order, rows, rights, part):
    return pl.pallas_call(
        half_kernel,
        grid_spec=pltpu.PrefetchScalarGridSpec(
            num_scalar_prefetch=1,
            grid=(1,),
            in_specs=[pl.BlockSpec((8, 2, 16, 2048), lambda i, o: (0, part, 0, 0))]
            + [pl.BlockSpec(memory_space=pl.ANY) for _ in rights],
            out_specs=pl.BlockSpec((8, 16, 16, 256), lambda i, o: (0, 0, 0, 0)),
            scratch_shapes=[pltpu.VMEM((2048, 2048), BF), pltpu.SemaphoreType.DMA((SLICES, 16))],
        ),
        out_shape=jax.ShapeDtypeStruct((8, 16, 16, 256), BF),
        compiler_params=pltpu.CompilerParams(vmem_limit_bytes=HALF << 20),
        name="half",
    )(order, rows, *rights)


def final_kernel(order, *refs):
    lefts, (columns, *_, out, rows, whole, arrived) = refs[:16], refs[16:]
    width = 2048 // SLICES
    copies = [
        [
            pltpu.make_async_copy(
                left.at[:, part * width : (part + 1) * width],
                whole.at[n * 128 : n * 128 + 128, part * width : (part + 1) * width],
                arrived.at[part, n],
            )
            for n, left in enumerate(lefts)
        ]
        for part in range(SLICES)
    ]
    for copy in sum(copies, []):
        copy.start()
    for n in range(len(lefts)):
        for chip in range(4):
            for p in range(2):
                top = n * 128 + chip * 32 + p * 16
                pair, place = order[2 * n] * 2 + p, order[2 * len(lefts) + (n // 4) * 4 + chip]
                rows[top : top + 16, :] = columns[pair, place]
    for part in range(SLICES):
        for copy in copies[part]:
            copy.wait()
        for top in range(part * width, (part + 1) * width, 512):
            total = lax.dot_general(
                whole[:, top : top + 512], rows[...], (((0,), (0,)), ((), ())), preferred_element_type=F32
            ).astype(BF)
            for t in range(2):
                out[t, top : top + 512] = total[:, t * 128 : t * 128 + 128]


def final_rotate(order, lefts, columns, part, begun=()):
    return pl.pallas_call(
        final_kernel,
        grid_spec=pltpu.PrefetchScalarGridSpec(
            num_scalar_prefetch=1,
            grid=(1,),
            in_specs=[pl.BlockSpec(memory_space=pl.ANY) for _ in lefts]
            + [pl.BlockSpec((8, 16, 16, 256), lambda i, o: (0, 0, 0, 0))]
            + [pl.BlockSpec(memory_space=pl.ANY) for _ in begun],
            out_specs=pl.BlockSpec((2, 2048, 128), lambda i, o: (part, 0, 0)),
            scratch_shapes=[
                pltpu.VMEM((2048, 256), BF),
                pltpu.VMEM((2048, 2048), BF),
                pltpu.SemaphoreType.DMA((SLICES, 16)),
            ],
        ),
        out_shape=jax.ShapeDtypeStruct((4, 2048, 128), BF),
        input_output_aliases={18: 0} if begun else {},
        compiler_params=pltpu.CompilerParams(vmem_limit_bytes=FINAL << 20),
        cost_estimate=pl.CostEstimate(flops=2 * 256 * 2048 * 2048, bytes_accessed=10 << 20, transcendentals=0),
        name="final",
    )(order, *lefts, columns, *begun)


def after(*values):
    return lax.optimization_barrier(values)


def shards(operators, left_rot, right_rot, integrals, pair_index, target_index):
    core = lax.axis_index("core")
    y, xl, z = lax.axis_index("y"), lax.axis_index("xl"), lax.axis_index("z")

    near = [right_rot] + [shift(right_rot, dz=dz) for dz in (1, -1, 2)]
    there = shift(right_rot, dx=1)
    pieces = operators.reshape(4, 8, 16, 2048).transpose(1, 0, 2, 3)
    pieces = lax.all_to_all(pieces, PAIR, 0, 0, tiled=True).reshape(512, 2048)
    spread = spread_coupling(integrals, pair_index, target_index)
    left_rot, there, spread = after(left_rot, there, spread)
    quarter = lax.dynamic_slice_in_dim(left_rot, y * 32, 32, 0)
    strip = jnp.concatenate([quarter, shift(quarter, dz=1), shift(quarter, dz=-1), shift(quarter, dz=2)])
    rights = near + [there, shift(there, dz=1), shift(there, dz=-1), shift(near[3], dx=1)]
    rights += [swap_core(right) for right in rights]
    rows = mix(spread, [pieces])
    rows, strip, *rights = after(rows.reshape(8, 4, 16, 2048), strip, *rights)
    lefts = [strip, shift(strip, dy=1), shift(strip, dy=-1)]
    across = [shift(strip, dx=1), shift(strip, dx=1, dy=1)]

    def along_z(xl, core):
        way = 1 - 2 * core
        return [(xl * 4 + chip % 4) * 2 + core for chip in (z, z + 4 - way, z + 4 + way, z + 2)]

    places = along_z(xl, core) + along_z(1 - xl, core) + along_z(xl, 1 - core) + along_z(1 - xl, 1 - core)
    def exchange(half):
        return lax.all_to_all(half.reshape(128, 16, 256), AXES, 0, 0, tiled=True).reshape(8, 16, 16, 256)

    places = jnp.stack(places)
    first = exchange(half_rotate(places, rows, rights, 0))
    rows, *lefts, across[0], across[1] = after(rows, *lefts, *across)
    half = half_rotate(places, rows, rights, 1)
    half, *lefts, across[0], across[1] = after(half, *lefts, *across)
    second = exchange(half)
    lefts.append(shift(lefts[1], dy=1))
    lefts += [across[0], across[1], shift(lefts[2], dx=1), shift(across[1], dy=1)]
    lefts += [swap_core(left) for left in lefts]
    order = jnp.concatenate([jnp.stack(left_order(y, core)), places])
    begun = final_rotate(order, lefts, first, 0)
    return final_rotate(order, lefts, second, 1, (begun,))


def left_order(y, core):
    order = []
    for side in (core, 1 - core):
        way = 1 - 2 * side
        for _ in range(2):
            for row in (y, (y + 4 - way) % 4, (y + 4 + way) % 4, (y + 2) % 4):
                order += [row, row]
    return order


def solution(mesh):
    fine = Mesh(mesh.devices.reshape(4, 2, 2, 4, 2), AXES)
    in_specs = (P(PAIR, MAT, None), P(MAT, None), P(MAT, None), P(), P(), P())
    out_specs = P(PAIR, None, MAT)
    return jax.shard_map(shards, mesh=fine, in_specs=in_specs, out_specs=out_specs, check_vma=False)
```

```python
import jax
import jax.numpy as jnp
from jax import lax
from jax.experimental import pallas as pl
from jax.experimental.pallas import tpu as pltpu
from jax.sharding import Mesh, PartitionSpec as P

AXES = ("y", "xh", "xl", "z", "core")
PAIR = ("y", "xh")
MAT = ("xl", "z", "core")
BF = jnp.bfloat16
F32 = jnp.float32
HALF, FINAL = 56, 16
SLICES = 1


def place(x, y, z, core):
    x, y, z = x % 4, y % 4, z % 4
    return (y * 2 + x // 2) * 16 + ((x % 2) * 4 + z) * 2 + core


def send(value, move):
    moves = [
        (place(x, y, z, core), place(*move(x, y, z, core)))
        for x in range(4)
        for y in range(4)
        for z in range(4)
        for core in range(2)
    ]
    return lax.ppermute(value, AXES, moves)


def swap_core(value):
    return send(value, lambda x, y, z, core: (x, y, z, 1 - core))


def shift(value, dx=0, dy=0, dz=0):
    def move(x, y, z, core):
        way = 1 - 2 * core
        return x + way * dx, y + way * dy, z + way * dz, core

    return send(value, move)


def selector(indices, count):
    return (indices[:, None] == jnp.arange(count, dtype=jnp.int32)[None, :]).astype(F32)


def spread_coupling(integrals, pair_index, target_index):
    npairs = integrals.shape[0]
    rowsel = jnp.dot(selector(target_index, npairs), integrals, precision=lax.Precision.HIGHEST)
    coupling = jnp.dot(rowsel, selector(pair_index, npairs).T, precision=lax.Precision.HIGHEST).astype(BF)
    wide = selector(jnp.arange(512, dtype=jnp.int32) // 16, 32).astype(BF)
    rows = jnp.dot(wide, coupling, preferred_element_type=F32).astype(BF)
    full = jnp.dot(rows, wide.T, preferred_element_type=F32).astype(BF)
    i = lax.broadcasted_iota(jnp.int32, (512, 512), 0) % 16
    j = lax.broadcasted_iota(jnp.int32, (512, 512), 1) % 16
    return jnp.where(i == j, full, jnp.zeros_like(full))


def mix_kernel(spread, *refs):
    *parts, out = refs
    width = out.shape[1] // len(parts)
    for n, part in enumerate(parts):
        out[:, n * width : (n + 1) * width] = jnp.dot(spread[...], part[...], preferred_element_type=F32).astype(BF)


def mix(spread, parts):
    return pl.pallas_call(
        mix_kernel,
        out_shape=jax.ShapeDtypeStruct((512, 2048), BF),
        compiler_params=pltpu.CompilerParams(vmem_limit_bytes=16 << 20),
        name="mix",
    )(spread, *parts)


def half_kernel(order, rows, *refs):
    rights, (out, natural, arrived) = refs[:16], refs[16:]
    width = 2048 // SLICES
    copies = [
        [
            pltpu.make_async_copy(
                right.at[:, part * width : (part + 1) * width],
                natural.at[pl.ds(pl.multiple_of(order[n] * 128, 128), 128), part * width : (part + 1) * width],
                arrived.at[part, n],
            )
            for n, right in enumerate(rights)
        ]
        for part in range(SLICES)
    ]
    for copy in sum(copies, []):
        copy.start()
    own = rows[...].reshape(256, 2048)
    for part in range(SLICES):
        for copy in copies[part]:
            copy.wait()
        for left in range(part * width, (part + 1) * width, 512):
            total = jnp.dot(own, natural[:, left : left + 512], preferred_element_type=F32).astype(BF)
            for p in range(8):
                for m in range(4):
                    for t in range(2):
                        top = (p * 2 + t) * 16
                        out[p, left // 128 + m, :, t * 128 : t * 128 + 128] = total[
                            top : top + 16, m * 128 : m * 128 + 128
                        ]


def half_rotate(order, rows, rights, part):
    return pl.pallas_call(
        half_kernel,
        grid_spec=pltpu.PrefetchScalarGridSpec(
            num_scalar_prefetch=1,
            grid=(1,),
            in_specs=[pl.BlockSpec((8, 2, 16, 2048), lambda i, o: (0, part, 0, 0))]
            + [pl.BlockSpec(memory_space=pl.ANY) for _ in rights],
            out_specs=pl.BlockSpec((8, 16, 16, 256), lambda i, o: (0, 0, 0, 0)),
            scratch_shapes=[pltpu.VMEM((2048, 2048), BF), pltpu.SemaphoreType.DMA((SLICES, 16))],
        ),
        out_shape=jax.ShapeDtypeStruct((8, 16, 16, 256), BF),
        compiler_params=pltpu.CompilerParams(vmem_limit_bytes=HALF << 20),
        name="half",
    )(order, rows, *rights)


def final_kernel(order, *refs):
    lefts, (columns, *_, out, rows, whole, arrived) = refs[:16], refs[16:]
    width = 2048 // SLICES
    copies = [
        [
            pltpu.make_async_copy(
                left.at[:, part * width : (part + 1) * width],
                whole.at[n * 128 : n * 128 + 128, part * width : (part + 1) * width],
                arrived.at[part, n],
            )
            for n, left in enumerate(lefts)
        ]
        for part in range(SLICES)
    ]
    for copy in sum(copies, []):
        copy.start()
    for n in range(len(lefts)):
        for chip in range(4):
            for p in range(2):
                top = n * 128 + chip * 32 + p * 16
                pair, place = order[2 * n] * 2 + p, order[2 * len(lefts) + (n // 4) * 4 + chip]
                rows[top : top + 16, :] = columns[pair, place]
    for part in range(SLICES):
        for copy in copies[part]:
            copy.wait()
        for top in range(part * width, (part + 1) * width, 512):
            total = lax.dot_general(
                whole[:, top : top + 512], rows[...], (((0,), (0,)), ((), ())), preferred_element_type=F32
            ).astype(BF)
            for t in range(2):
                out[t, top : top + 512] = total[:, t * 128 : t * 128 + 128]


def final_rotate(order, lefts, columns, part, begun=()):
    return pl.pallas_call(
        final_kernel,
        grid_spec=pltpu.PrefetchScalarGridSpec(
            num_scalar_prefetch=1,
            grid=(1,),
            in_specs=[pl.BlockSpec(memory_space=pl.ANY) for _ in lefts]
            + [pl.BlockSpec((8, 16, 16, 256), lambda i, o: (0, 0, 0, 0))]
            + [pl.BlockSpec(memory_space=pl.ANY) for _ in begun],
            out_specs=pl.BlockSpec((2, 2048, 128), lambda i, o: (part, 0, 0)),
            scratch_shapes=[
                pltpu.VMEM((2048, 256), BF),
                pltpu.VMEM((2048, 2048), BF),
                pltpu.SemaphoreType.DMA((SLICES, 16)),
            ],
        ),
        out_shape=jax.ShapeDtypeStruct((4, 2048, 128), BF),
        input_output_aliases={18: 0} if begun else {},
        compiler_params=pltpu.CompilerParams(vmem_limit_bytes=FINAL << 20),
        cost_estimate=pl.CostEstimate(flops=2 * 256 * 2048 * 2048, bytes_accessed=10 << 20, transcendentals=0),
        name="final",
    )(order, *lefts, columns, *begun)


def after(*values):
    return lax.optimization_barrier(values)


def shards(operators, left_rot, right_rot, integrals, pair_index, target_index):
    core = lax.axis_index("core")
    y, xl, z = lax.axis_index("y"), lax.axis_index("xl"), lax.axis_index("z")

    near = [right_rot] + [shift(right_rot, dz=dz) for dz in (1, -1, 2)]
    there = shift(right_rot, dx=1)
    pieces = operators.reshape(4, 8, 16, 2048).transpose(1, 0, 2, 3)
    pieces = lax.all_to_all(pieces, PAIR, 0, 0, tiled=True).reshape(512, 2048)
    spread = spread_coupling(integrals, pair_index, target_index)
    left_rot, there, spread = after(left_rot, there, spread)
    quarter = lax.dynamic_slice_in_dim(left_rot, y * 32, 32, 0)
    strip = jnp.concatenate([quarter, shift(quarter, dz=1), shift(quarter, dz=-1), shift(quarter, dz=2)])
    rights = near + [there, shift(there, dz=1), shift(there, dz=-1), shift(near[3], dx=1)]
    rights += [swap_core(right) for right in rights]
    rows = mix(spread, [pieces])
    rows, strip, *rights = after(rows.reshape(8, 4, 16, 2048), strip, *rights)
    lefts = [strip, shift(strip, dy=1), shift(strip, dy=-1)]
    across = [shift(strip, dx=1), shift(strip, dx=1, dy=1)]

    def along_z(xl, core):
        way = 1 - 2 * core
        return [(xl * 4 + chip % 4) * 2 + core for chip in (z, z + 4 - way, z + 4 + way, z + 2)]

    places = along_z(xl, core) + along_z(1 - xl, core) + along_z(xl, 1 - core) + along_z(1 - xl, 1 - core)
    def exchange(half):
        return lax.all_to_all(half.reshape(128, 16, 256), AXES, 0, 0, tiled=True).reshape(8, 16, 16, 256)

    places = jnp.stack(places)
    first = exchange(half_rotate(places, rows, rights, 0))
    rows, *lefts, across[0], across[1] = after(rows, *lefts, *across)
    half = half_rotate(places, rows, rights, 1)
    half, *lefts, across[0], across[1] = after(half, *lefts, *across)
    second = exchange(half)
    lefts.append(shift(lefts[1], dy=1))
    lefts += [across[0], across[1], shift(lefts[2], dx=1), shift(across[1], dy=1)]
    lefts += [swap_core(left) for left in lefts]
    order = jnp.concatenate([jnp.stack(left_order(y, core)), places])
    begun = final_rotate(order, lefts, first, 0)
    return final_rotate(order, lefts, second, 1, (begun,))


def left_order(y, core):
    order = []
    for side in (core, 1 - core):
        way = 1 - 2 * side
        for _ in range(2):
            for row in (y, (y + 4 - way) % 4, (y + 4 + way) % 4, (y + 2) % 4):
                order += [row, row]
    return order


def solution(mesh):
    fine = Mesh(mesh.devices.reshape(4, 2, 2, 4, 2), AXES)
    in_specs = (P(PAIR, MAT, None), P(MAT, None), P(MAT, None), P(), P(), P())
    out_specs = P(PAIR, None, MAT)
    return jax.shard_map(shards, mesh=fine, in_specs=in_specs, out_specs=out_specs, check_vma=False)
```
